32 devices in a mesh: groups: 2 (over y), ctx: 4 (over z), tp: 2 (over x), sub: 2 (over core).
Axes of the slice: x: 2, y: 2, z: 4, core: 2. Of those that a mesh axis runs over, the one named last changes fastest.
Arguments:
- queries: bfloat16 [4096, 8192], P(('groups', 'ctx'), ('tp', 'sub')), parts along dimension 0, may hold values from -6 to 6
- prompt_kv: bfloat16 [4096, 2048], P(('groups', 'ctx'), ('tp', 'sub')), parts along dimension 0, may hold values from -6 to 6
- resp_kv: bfloat16 [4096, 2048], P(('groups', 'ctx'), ('tp', 'sub')), parts along dimension 0, may hold values from -6 to 6
- block_resp: int32 [16], P('groups'), parts along dimension 0, may hold values from 0 to 3, as said below
- block_pos: int32 [16], P('groups'), parts along dimension 0, may hold values from 0 to 3
Outputs:
- attended: bfloat16 [4096, 8192], P(('groups', 'ctx'), ('tp', 'sub')), parts along dimension 0
The draws below stay inside these ranges and needn't reach their ends.
There are 2 independent parts, one for each index of `groups`. The reference program is written for one: setup_inputs(seed, part) draws one part's arguments, and reference() takes and returns one part's arrays. A program takes and returns all parts, laid end to end along the dimension named above; each array names one. Nothing has to cross between parts.
Inputs may be any that keep to these rules, and one draw needn't show every extreme that they name: block_resp and block_pos place every block of every response in exactly one slot: response r has a length of 1 to 4 blocks, some response exactly 4, and one slot for each of its positions 0 to its length - 1; response r belongs to prompt r // 4.
All inputs are finite; a program needn't handle non-finite values.
Results may differ from the reference program's by a relative error of at most 0.0065.
Values may be sent and summed in bfloat16 or wider, within the bound.
A program may use at most 128 MiB of HBM per device.

```python
import math
import jax
import jax.numpy as jnp
from jax import lax

HD = 128
QH = 64
KVH = 8
BLK = 256
PLEN = 2048
GEN = 4
MAXB = 4
PROMPTS = 1
NRESP = 4
NBLK = 8


def layout(key):
    extra = NBLK - NRESP - (MAXB - 1)
    key_big, key_tick, key_perm = jax.random.split(key, 3)
    big = jax.random.randint(key_big, (), 0, NRESP)
    tickets = jax.random.permutation(key_tick, (NRESP - 1) * (MAXB - 1))[:extra]
    owners = tickets // (MAXB - 1)
    others = jnp.sum((owners[:, None] == jnp.arange(NRESP - 1)[None, :]).astype(jnp.int32), axis=0)
    index = jnp.arange(NRESP)
    other_index = jnp.clip(index - (index > big).astype(jnp.int32), 0, NRESP - 2)
    lengths = jnp.where(index == big, MAXB, 1 + others[other_index])
    ends = jnp.cumsum(lengths)
    starts = ends - lengths
    order = jax.random.permutation(key_perm, NBLK)
    resp = jnp.sum((ends[None, :] <= order[:, None]).astype(jnp.int32), axis=1)
    pos = order - starts[resp]
    return (resp.astype(jnp.int32), pos.astype(jnp.int32))


def draw_block_resp(key, part):
    return layout(key)[0]


def draw_block_pos(key, part):
    return layout(key)[1]


def draw_queries(key, part):
    key = jax.random.fold_in(key, 3)
    nrow = NBLK * BLK
    ncol = QH * HD
    out = jnp.clip(jax.random.normal(key, (nrow, ncol)), -6.0, 6.0)
    return out.astype(jnp.bfloat16)


def draw_prompt_kv(key, part):
    key = jax.random.fold_in(key, 5)
    nrow = PROMPTS * PLEN
    ncol = 2 * KVH * HD
    out = jnp.clip(jax.random.normal(key, (nrow, ncol)), -6.0, 6.0)
    return out.astype(jnp.bfloat16)


def shard_levels(stream_key, shape, pieces, least, top_value):
    loudness, own = 1.0, jax.random.fold_in(stream_key, 6)
    for axis_at, parts in pieces:
        heights = jnp.exp(jax.random.uniform(jax.random.fold_in(own, axis_at), (parts,), jnp.float32, least / len(pieces), top_value / len(pieces)))
        loudness = loudness * jnp.repeat(heights, shape[axis_at] // parts).reshape([-1 if axis == axis_at else 1 for axis in range(len(shape))])
    return loudness


def gaussian(stream_key, shape, spread, bound, cuts=(), kind=jnp.bfloat16):
    array = jax.random.normal(stream_key, shape, jnp.float32) * spread
    if len(cuts) > 0:
        array = shard_levels(stream_key, shape, cuts, -0.22, 0.18) * array
    return jnp.clip(array, min=-bound, max=bound).astype(kind)


def setup_inputs(seed: int = 0, part: int = 0) -> dict:
    key_list = jax.random.split(jax.random.key(seed), 6)
    part_splits = jax.random.split(jax.random.fold_in(key_list[5], part), 6)
    queries = draw_queries(jax.random.fold_in(jax.random.fold_in(key_list[5], part), 71), part)
    prompt_kv = draw_prompt_kv(jax.random.fold_in(jax.random.fold_in(key_list[5], part), 71), part)
    resp_kv = gaussian(part_splits[2], (NBLK * BLK, 2 * KVH * HD), 1.0, 6.0, ((0, 4), (1, 4)))
    block_resp = draw_block_resp(jax.random.fold_in(jax.random.fold_in(key_list[5], part), 71), part)
    block_pos = draw_block_pos(jax.random.fold_in(jax.random.fold_in(key_list[5], part), 71), part)
    return {"queries": queries, "prompt_kv": prompt_kv, "resp_kv": resp_kv, "block_resp": block_resp, "block_pos": block_pos}


def reference(queries, prompt_kv, resp_kv, block_resp, block_pos):
    group = QH // KVH
    scale = 1.0 / math.sqrt(HD)
    keylen = PLEN + MAXB * BLK
    resp_blocks = resp_kv.reshape(NBLK, BLK, 2 * KVH * HD)
    positions = jnp.arange(MAXB, dtype=jnp.int32)
    slot_ids = jnp.arange(NBLK, dtype=jnp.int32)
    row_ids = jnp.arange(BLK, dtype=jnp.int32)
    which = jnp.repeat(positions, BLK)
    inner = jnp.tile(row_ids, MAXB)

    def one_block(slot):
        resp = block_resp[slot]
        pos = block_pos[slot]
        prompt = resp // GEN
        hit = (block_resp[None, :] == resp) & (block_pos[None, :] == positions[:, None])
        table = lax.optimization_barrier(jnp.sum(jnp.where(hit, slot_ids[None, :], 0), axis=1)).astype(jnp.int32)
        prompt_rows = lax.dynamic_slice_in_dim(prompt_kv, (prompt * PLEN).astype(jnp.int32), PLEN, 0)
        answer_rows = resp_blocks[table].reshape(MAXB * BLK, 2 * KVH * HD)
        keyvals = jnp.concatenate([prompt_rows, answer_rows], axis=0).reshape(keylen, KVH, 2, HD).astype(jnp.float32)
        keys = keyvals[:, :, 0]
        values = keyvals[:, :, 1]
        query = lax.dynamic_slice_in_dim(queries, (slot * BLK).astype(jnp.int32), BLK, 0)
        query = query.reshape(BLK, KVH, group, HD).astype(jnp.float32)
        scores = jnp.einsum('tkgd,lkd->kgtl', query, keys) * scale
        answer_mask = (which[None, :] < pos) | (which[None, :] == pos) & (inner[None, :] <= row_ids[:, None])
        mask = jnp.concatenate([jnp.ones((BLK, PLEN), dtype=bool), answer_mask], axis=1)
        scores = jnp.where(mask[None, None], scores, -1e+30)
        peak = lax.optimization_barrier(jnp.max(scores, axis=-1, keepdims=True))
        expo = jnp.exp(scores - peak)
        total = lax.optimization_barrier(jnp.sum(expo, axis=-1, keepdims=True))
        probs = lax.optimization_barrier(expo.astype(jnp.bfloat16)).astype(jnp.float32)
        mixed = jnp.einsum('kgtl,lkd->kgtd', probs, values) / total
        return mixed.transpose(2, 0, 1, 3).reshape(BLK, QH * HD).astype(jnp.bfloat16)
    out = lax.map(one_block, jnp.arange(NBLK, dtype=jnp.int32))
    return out.reshape(NBLK * BLK, QH * HD)
```

```python
import math

import jax
import jax.numpy as jnp
from jax import lax
from jax.experimental import pallas as pl
from jax.experimental.pallas import tpu as pltpu
from jax.sharding import PartitionSpec as P

HD = 128
QH = 64
KVH = 8
BLK = 256
PLEN = 2048
GEN = 4
MAXB = 4


def shards(queries, prompt_kv, resp_kv, block_resp, block_pos):
    rows = queries.shape[0]
    nloc = rows // BLK
    width = prompt_kv.shape[1]
    kvloc = width // (2 * HD)
    group = QH // KVH
    qloc = kvloc * group
    nblk = block_resp.shape[0]
    scale = 1.0 / math.sqrt(HD)
    slots_here = lax.axis_index("ctx") * nloc + jnp.arange(nloc, dtype=jnp.int32)
    resp_here = block_resp[slots_here]
    pos_here = block_pos[slots_here]
    qheads = queries.reshape(nloc, BLK, qloc, HD).transpose(2, 0, 1, 3)
    within = jnp.arange(BLK, dtype=jnp.int32)
    all_prompt, all_answer = (
        lax.all_gather(prompt_kv, "ctx", axis=0, tiled=True),
        lax.all_gather(resp_kv, "ctx", axis=0, tiled=True),
    )
    answer_blocks = all_answer.reshape(nblk, BLK, width)
    positions = jnp.arange(MAXB, dtype=jnp.int32)
    hit = (block_resp[None, None, :] == resp_here[:, None, None]) & (
        block_pos[None, None, :] == positions[None, :, None]
    )
    table = jnp.sum(jnp.where(hit, jnp.arange(nblk, dtype=jnp.int32)[None, None, :], 0), axis=-1)
    prompt_rows = jnp.stack(
        [
            lax.dynamic_slice_in_dim(all_prompt, resp_here[slot] // GEN * PLEN, PLEN, 0)
            for slot in range(nloc)
        ]
    )
    answer_rows = answer_blocks[table].reshape(nloc, MAXB * BLK, width)
    keyvals = jnp.concatenate([prompt_rows, answer_rows], axis=1).reshape(
        nloc, PLEN + MAXB * BLK, kvloc, 2, HD
    )
    keys = keyvals[:, :, :, 0].transpose(2, 0, 1, 3)
    values = keyvals[:, :, :, 1].transpose(2, 0, 1, 3)
    which = jnp.repeat(positions, BLK)
    inner = jnp.tile(within, MAXB)
    answer_mask = (which[None, None, :] < pos_here[:, None, None]) | (
        which[None, None, :] == pos_here[:, None, None]
    ) & (inner[None, None, :] <= within[None, :, None])
    mask = jnp.concatenate([jnp.ones((nloc, BLK, PLEN), dtype=bool), answer_mask], axis=2)

    def one_head(index):
        owner = index // group
        scores = (
            jnp.einsum(
                "btd,bld->btl", qheads[index], keys[owner], preferred_element_type=jnp.float32
            )
            * scale
        )
        scores = jnp.where(mask, scores, -1e30)
        peak = jnp.max(scores, axis=-1, keepdims=True)
        expo = jnp.exp(scores - peak)
        total = jnp.sum(expo, axis=-1, keepdims=True)
        probs = expo.astype(jnp.bfloat16)
        mixed = (
            jnp.einsum("btl,bld->btd", probs, values[owner], preferred_element_type=jnp.float32)
            / total
        )
        return mixed.astype(jnp.bfloat16)

    outputs = lax.map(one_head, jnp.arange(qloc, dtype=jnp.int32))
    return outputs.transpose(1, 2, 0, 3).reshape(rows, qloc * HD)


NT = (((1,), (1,)), ((), ()))
TN = (((0,), (0,)), ((), ()))
C2 = math.log2(math.e) / math.sqrt(HD)
MESH = pl.DeviceIdType.MESH


def kernel(
    q_ref, p_ref, r_ref, resp_ref, pos_ref, o_ref,
    pb, rb, eb, fb, q2, acc, m, l,
    recv_p, recv_r, recv_e, send_e, send_o,
):
    me = lax.axis_index("ctx")
    is_end = (me == 0) | (me == 3)
    is_mid = (me == 1) | (me == 2)
    low = me < 2
    near = jnp.where(low, 0, 3)
    other = jnp.where(low, 2, 1)
    far = 3 - near
    inner = jnp.where(me == 0, 1, jnp.where(me == 3, 2, other))

    def p_at(src, half):
        return pb.at[src, pl.ds(half * BLK, BLK)]

    def p_copy(src, half, sem, to):
        return pltpu.make_async_remote_copy(
            src_ref=p_at(src, half), dst_ref=p_at(src, half), send_sem=sem,
            recv_sem=recv_p.at[src, half], device_id={"ctx": to}, device_id_type=MESH,
        )

    def r_copy(src, half, sem, to):
        return pltpu.make_async_remote_copy(
            src_ref=rb.at[src, half], dst_ref=rb.at[src, half], send_sem=sem,
            recv_sem=recv_r.at[src, half], device_id={"ctx": to}, device_id_type=MESH,
        )

    def e_copy(k, sem, to):
        return pltpu.make_async_remote_copy(
            src_ref=eb.at[k], dst_ref=eb.at[k], send_sem=sem,
            recv_sem=recv_e.at[k], device_id={"ctx": to}, device_id_type=MESH,
        )

    def got_p(src, half):
        p_copy(src, half, send_o.at[0], inner).wait_recv()

    def got_r(src, half):
        r_copy(src, half, send_o.at[0], inner).wait_recv()

    def got_e(k):
        e_copy(k, send_o.at[0], inner).wait_recv()

    def own_p(half, sem, to):
        return p_copy(me, half, sem, to)

    barrier = pltpu.get_barrier_semaphore()
    pl.semaphore_signal(barrier, inc=1, device_id={"ctx": inner}, device_id_type=MESH)

    @pl.when(is_mid)
    def _():
        pl.semaphore_signal(barrier, inc=1, device_id={"ctx": near}, device_id_type=MESH)

    pb[me] = p_ref[...]
    rb[me, 0] = r_ref[:BLK]
    rb[me, 1] = r_ref[BLK:]

    @pl.when(is_mid)
    def _():
        pl.semaphore_wait(barrier, 2)

    @pl.when(is_end)
    def _():
        pl.semaphore_wait(barrier, 1)

    @pl.when(is_mid)
    def _():
        for half in range(2):
            own_p(half, send_e.at[half], near).start()

    for half in range(2):
        own_p(half, send_o.at[half], inner).start()
    for half in range(2):
        r_copy(me, half, send_o.at[2 + half], inner).start()

    def needs(target, cand):
        same = resp_ref[target] == resp_ref[cand]
        return jnp.where(same & (pos_ref[cand] < pos_ref[target]), 1, 0)

    def right_aligned(flags, count):
        after = 0
        ranks = []
        for flag in reversed(flags):
            ranks.append(count - 1 - after)
            after = after + flag
        ranks.reverse()
        return [
            [jnp.where(ranks[i] == k, flags[i], 0) for i in range(len(flags))]
            for k in range(count)
        ]

    def choose(pick, blocks):
        out = blocks[0]
        for i in range(1, len(blocks)):
            out = lax.select_n(pick[i] == 1, out, blocks[i])
        return out

    def end_picks(end, first, second, third):
        cands = [2 * first, 2 * first + 1, 2 * second, 2 * second + 1, 2 * third, 2 * third + 1]
        flags = [jnp.maximum(needs(2 * end, c), needs(2 * end + 1, c)) for c in cands]
        return cands, right_aligned(flags, 4)

    def send_entry(k, sem):
        order = (me, other, far)
        _, picks = end_picks(near, *order)
        blocks = [rb[src, half] for src in order for half in range(2)][: k + 3]
        eb[k] = choose(picks[k], blocks)
        e_copy(k, sem, near).start()

    def attend(k, v, base, bias=None, diag=False):
        keys = k.shape[0]
        k2 = jnp.concatenate([k, k], axis=1)
        scores = [
            lax.dot_general(k2, q2[base + u], NT, preferred_element_type=jnp.float32)
            for u in range(QH // KVH)
        ]
        if diag:
            key_at = lax.broadcasted_iota(jnp.int32, (keys, BLK), 0)
            row_at = lax.broadcasted_iota(jnp.int32, (keys, BLK), 1)
            seen = key_at <= row_at
        for u, s in enumerate(scores):
            i = base + u
            if diag:
                s = jnp.where(seen, s, -1e30)
            peak = jnp.max(s, axis=0, keepdims=True)
            if diag:
                expo = jnp.exp2(s - peak)
                l[i, 0:1] = jnp.sum(expo, axis=0, keepdims=True)
                m[i, 0:1] = peak
                acc[i] = lax.dot_general(
                    v, expo.astype(jnp.bfloat16), TN, preferred_element_type=jnp.float32
                )
            else:
                before = m[i, 0:1]
                if bias is not None:
                    peak = peak - bias
                peak = jnp.maximum(before, peak)
                expo = jnp.exp2(s - (peak if bias is None else peak + bias))
                decay = jnp.exp2(before - peak)
                l[i, 0:1] = l[i, 0:1] * decay + jnp.sum(expo, axis=0, keepdims=True)
                m[i, 0:1] = peak
                acc[i] = acc[i] * decay + lax.dot_general(
                    v, expo.astype(jnp.bfloat16), TN, preferred_element_type=jnp.float32
                )

    def columns(head):
        return (
            pl.ds(pl.multiple_of(head * 2 * HD, 2 * HD), HD),
            pl.ds(pl.multiple_of(head * 2 * HD + HD, HD), HD),
        )

    def q_at(i):
        slot, head = i // 16, i % 16
        return (
            pl.ds(pl.multiple_of(slot * BLK, BLK), BLK),
            pl.ds(pl.multiple_of(head * HD, HD), HD),
        )

    @pl.loop(0, 32)
    def _(i):
        rows, cols = q_at(i)
        scaled = q_ref[rows, cols].astype(jnp.float32) * C2
        high = scaled.astype(jnp.bfloat16)
        rest = (scaled - high.astype(jnp.float32)).astype(jnp.bfloat16)
        q2[i] = jnp.concatenate([high, rest], axis=1)

    @pl.loop(0, 4)
    def _(it):
        slot, head = it // 2, it % 2
        kc, vc = columns(head)
        rows = pl.ds(pl.multiple_of(slot * BLK, BLK), BLK)
        attend(r_ref[rows, kc], r_ref[rows, vc], slot * 16 + head * 8, diag=True)

    def at(it, tick, role, action):
        pl.when((it == tick) & role)(action)

    def pass_p(src, half, sem, to):
        def go():
            got_p(src, half)
            p_copy(src, half, sem, to).start()
        return go

    def pass_r(src, half, sem, to):
        def go():
            got_r(src, half)
            r_copy(src, half, sem, to).start()
        return go

    def take_entry(half, k, sem, src):
        def go():
            got_r(src, half)
            send_entry(k, sem)
        return go

    def take_p(src):
        def go():
            got_p(src, 0)
            got_p(src, 1)
        return go

    def prompt_step(it):
        step = it // 4
        second = jnp.where(low, 1 - me, 5 - me)
        third = jnp.where(low, 2, 1)
        fourth = jnp.where(low, 3, 0)
        src = jnp.where(
            step == 0, me, jnp.where(step == 1, second, jnp.where(step == 2, third, fourth))
        )
        at(it, 1, is_mid, pass_p(other, 0, send_e.at[2], near))
        at(it, 1, is_mid, pass_p(near, 0, send_o.at[4], other))
        at(it, 4, is_mid, pass_p(other, 1, send_e.at[3], near))
        at(it, 4, is_mid, pass_p(near, 1, send_o.at[5], other))
        at(it, 6, is_mid, take_entry(0, 0, send_e.at[4], other))
        at(it, 7, is_mid, pass_r(near, 0, send_o.at[6], other))
        at(it, 9, is_mid, take_entry(1, 1, send_e.at[5], other))
        at(it, 9, is_mid, pass_r(near, 1, send_o.at[7], other))
        at(it, 11, is_mid, pass_p(far, 0, send_e.at[6], near))
        at(it, 12, is_mid, pass_p(far, 1, send_e.at[7], near))
        at(it, 4, is_end, take_p(second))
        at(it, 8, is_end, take_p(third))
        at(it, 12, is_end, take_p(fourth))
        slot, head = (it % 4) // 2, it % 2
        kc, vc = columns(head)
        attend(pb[src, :, kc], pb[src, :, vc], slot * 16 + head * 8)

    def fill(k):
        used = []
        for slot in range(2):
            mine, sib = 2 * me + slot, 2 * me + 1 - slot

            order = (near, other, far)
            cands = [2 * src + half for src in order for half in range(2)]
            flags = [needs(mine, sib)] + [needs(mine, c) for c in cands]
            mid_pick = right_aligned(flags, 3)[k]

            ends, picks = end_picks(me, inner, jnp.where(low, 2, 1), jnp.where(low, 3, 0))
            flags = [needs(mine, sib)]
            for entry in range(4):
                flag = 0
                for i, c in enumerate(ends):
                    flag = flag + picks[entry][i] * needs(mine, c)
                flags.append(flag)
            end_pick = right_aligned(flags, 3)[k]

            def fill_mid():
                blocks = [rb[me, 1 - slot]]
                blocks += [rb[src, half] for src in order for half in range(2)][: k + 4]
                fb[slot] = choose(mid_pick, blocks)

            def fill_end():
                blocks = [rb[me, 1 - slot]] + [eb[entry] for entry in range(k + 2)]
                fb[slot] = choose(end_pick, blocks)

            pl.when(is_mid)(fill_mid)
            pl.when(is_end)(fill_end)
            used.append(jnp.where(is_mid, sum(mid_pick), sum(end_pick)))
        biases = [jnp.where(u == 1, 0.0, 1e30).astype(jnp.float32) for u in used]

        @pl.loop(0, 4)
        def _(it):
            slot, head = it // 2, it % 2
            kc, vc = columns(head)
            bias = jnp.where(slot == 0, biases[0], biases[1])
            attend(fb[slot, :, kc], fb[slot, :, vc], slot * 16 + head * 8, bias=bias)

    pl.loop(0, 12)(prompt_step)

    @pl.when(is_end)
    def _():
        got_e(0)
        got_e(1)

    fill(0)
    pl.loop(12, 16)(prompt_step)
    pl.when(is_mid)(take_entry(0, 2, send_e.at[8], far))
    pl.when(is_end)(lambda: got_e(2))
    fill(1)
    pl.when(is_mid)(take_entry(1, 3, send_e.at[9], far))
    pl.when(is_end)(lambda: got_e(3))
    fill(2)

    @pl.loop(0, 32)
    def _(i):
        rows, cols = q_at(i)
        o_ref[rows, cols] = (acc[i] / l[i, 0:1]).T.astype(o_ref.dtype)

    for half in range(2):
        own_p(half, send_o.at[half], inner).wait_send()
        r_copy(me, half, send_o.at[2 + half], inner).wait_send()

    @pl.when(is_mid)
    def _():
        for half in range(2):
            own_p(half, send_e.at[half], near).wait_send()
            p_copy(other, half, send_e.at[2 + half], near).wait_send()
            e_copy(half, send_e.at[4 + half], near).wait_send()
            p_copy(far, half, send_e.at[6 + half], near).wait_send()
            e_copy(2 + half, send_e.at[8 + half], near).wait_send()
            p_copy(near, half, send_o.at[4 + half], other).wait_send()
            r_copy(near, half, send_o.at[6 + half], other).wait_send()


def line_of_four(queries, prompt_kv, resp_kv, block_resp, block_pos):
    rows, cols = queries.shape
    width = prompt_kv.shape[1]
    vmem = pl.BlockSpec(memory_space=pltpu.VMEM)
    smem = pl.BlockSpec(memory_space=pltpu.SMEM)
    heads = cols // HD
    tiles = rows // BLK * heads
    return pl.pallas_call(
        kernel,
        out_shape=jax.ShapeDtypeStruct((rows, cols), jnp.bfloat16),
        in_specs=[vmem, vmem, vmem, smem, smem],
        out_specs=vmem,
        scratch_shapes=[
            pltpu.VMEM((4, 2 * BLK, width), jnp.bfloat16),
            pltpu.VMEM((4, 2, BLK, width), jnp.bfloat16),
            pltpu.VMEM((4, BLK, width), jnp.bfloat16),
            pltpu.VMEM((2, BLK, width), jnp.bfloat16),
            pltpu.VMEM((tiles, BLK, 2 * HD), jnp.bfloat16),
            pltpu.VMEM((tiles, HD, BLK), jnp.float32),
            pltpu.VMEM((tiles, 8, BLK), jnp.float32),
            pltpu.VMEM((tiles, 8, BLK), jnp.float32),
            pltpu.SemaphoreType.DMA((4, 2)),
            pltpu.SemaphoreType.DMA((4, 2)),
            pltpu.SemaphoreType.DMA((4,)),
            pltpu.SemaphoreType.DMA((10,)),
            pltpu.SemaphoreType.DMA((8,)),
        ],
        compiler_params=pltpu.CompilerParams(
            collective_id=0, has_side_effects=True, vmem_limit_bytes=56 * 2**20
        ),
        name="line_attention",
    )(queries, prompt_kv, resp_kv, block_resp, block_pos)


def shards_of(queries, prompt_kv, resp_kv, block_resp, block_pos):
    ctx = lax.axis_size("ctx")
    fits = (
        ctx == 4
        and queries.shape == (2 * BLK, 2 * (QH // KVH) * HD)
        and prompt_kv.shape == (PLEN // 4, 4 * HD)
        and resp_kv.shape == (2 * BLK, 4 * HD)
    )
    run = line_of_four if fits else shards
    return run(queries, prompt_kv, resp_kv, block_resp, block_pos)


def solution(mesh):
    in_specs = (
        P(("groups", "ctx"), ("tp", "sub")),
        P(("groups", "ctx"), ("tp", "sub")),
        P(("groups", "ctx"), ("tp", "sub")),
        P("groups"),
        P("groups"),
    )
    out_specs = P(("groups", "ctx"), ("tp", "sub"))
    return jax.shard_map(shards_of, mesh=mesh, in_specs=in_specs, out_specs=out_specs, check_vma=False)
```

```python
import math

import jax
import jax.numpy as jnp
from jax import lax
from jax.experimental import pallas as pl
from jax.experimental.pallas import tpu as pltpu
from jax.sharding import PartitionSpec as P

HD = 128
QH = 64
KVH = 8
BLK = 256
PLEN = 2048
GEN = 4
MAXB = 4


def shards(queries, prompt_kv, resp_kv, block_resp, block_pos):
    rows = queries.shape[0]
    nloc = rows // BLK
    width = prompt_kv.shape[1]
    kvloc = width // (2 * HD)
    group = QH // KVH
    qloc = kvloc * group
    nblk = block_resp.shape[0]
    scale = 1.0 / math.sqrt(HD)
    slots_here = lax.axis_index("ctx") * nloc + jnp.arange(nloc, dtype=jnp.int32)
    resp_here = block_resp[slots_here]
    pos_here = block_pos[slots_here]
    qheads = queries.reshape(nloc, BLK, qloc, HD).transpose(2, 0, 1, 3)
    within = jnp.arange(BLK, dtype=jnp.int32)
    all_prompt, all_answer = (
        lax.all_gather(prompt_kv, "ctx", axis=0, tiled=True),
        lax.all_gather(resp_kv, "ctx", axis=0, tiled=True),
    )
    answer_blocks = all_answer.reshape(nblk, BLK, width)
    positions = jnp.arange(MAXB, dtype=jnp.int32)
    hit = (block_resp[None, None, :] == resp_here[:, None, None]) & (
        block_pos[None, None, :] == positions[None, :, None]
    )
    table = jnp.sum(jnp.where(hit, jnp.arange(nblk, dtype=jnp.int32)[None, None, :], 0), axis=-1)
    prompt_rows = jnp.stack(
        [
            lax.dynamic_slice_in_dim(all_prompt, resp_here[slot] // GEN * PLEN, PLEN, 0)
            for slot in range(nloc)
        ]
    )
    answer_rows = answer_blocks[table].reshape(nloc, MAXB * BLK, width)
    keyvals = jnp.concatenate([prompt_rows, answer_rows], axis=1).reshape(
        nloc, PLEN + MAXB * BLK, kvloc, 2, HD
    )
    keys = keyvals[:, :, :, 0].transpose(2, 0, 1, 3)
    values = keyvals[:, :, :, 1].transpose(2, 0, 1, 3)
    which = jnp.repeat(positions, BLK)
    inner = jnp.tile(within, MAXB)
    answer_mask = (which[None, None, :] < pos_here[:, None, None]) | (
        which[None, None, :] == pos_here[:, None, None]
    ) & (inner[None, None, :] <= within[None, :, None])
    mask = jnp.concatenate([jnp.ones((nloc, BLK, PLEN), dtype=bool), answer_mask], axis=2)

    def one_head(index):
        owner = index // group
        scores = (
            jnp.einsum(
                "btd,bld->btl", qheads[index], keys[owner], preferred_element_type=jnp.float32
            )
            * scale
        )
        scores = jnp.where(mask, scores, -1e30)
        peak = jnp.max(scores, axis=-1, keepdims=True)
        expo = jnp.exp(scores - peak)
        total = jnp.sum(expo, axis=-1, keepdims=True)
        probs = expo.astype(jnp.bfloat16)
        mixed = (
            jnp.einsum("btl,bld->btd", probs, values[owner], preferred_element_type=jnp.float32)
            / total
        )
        return mixed.astype(jnp.bfloat16)

    outputs = lax.map(one_head, jnp.arange(qloc, dtype=jnp.int32))
    return outputs.transpose(1, 2, 0, 3).reshape(rows, qloc * HD)


NT = (((1,), (1,)), ((), ()))
TN = (((0,), (0,)), ((), ()))
C2 = math.log2(math.e) / math.sqrt(HD)
MESH = pl.DeviceIdType.MESH


def kernel(
    q_ref, p_ref, r_ref, resp_ref, pos_ref, o_ref,
    pb, rb, eb, fb, q2, acc, m, l,
    recv_p, recv_r, recv_e, send_e, send_o,
):
    me = lax.axis_index("ctx")
    is_end = (me == 0) | (me == 3)
    is_mid = (me == 1) | (me == 2)
    low = me < 2
    near = jnp.where(low, 0, 3)
    other = jnp.where(low, 2, 1)
    far = 3 - near
    inner = jnp.where(me == 0, 1, jnp.where(me == 3, 2, other))

    def p_at(src, half):
        return pb.at[src, pl.ds(half * BLK, BLK)]

    def p_copy(src, half, sem, to):
        return pltpu.make_async_remote_copy(
            src_ref=p_at(src, half), dst_ref=p_at(src, half), send_sem=sem,
            recv_sem=recv_p.at[src, half], device_id={"ctx": to}, device_id_type=MESH,
        )

    def r_copy(src, half, sem, to):
        return pltpu.make_async_remote_copy(
            src_ref=rb.at[src, half], dst_ref=rb.at[src, half], send_sem=sem,
            recv_sem=recv_r.at[src, half], device_id={"ctx": to}, device_id_type=MESH,
        )

    def e_copy(k, sem, to):
        return pltpu.make_async_remote_copy(
            src_ref=eb.at[k], dst_ref=eb.at[k], send_sem=sem,
            recv_sem=recv_e.at[k], device_id={"ctx": to}, device_id_type=MESH,
        )

    def got_p(src, half):
        p_copy(src, half, send_o.at[0], inner).wait_recv()

    def got_r(src, half):
        r_copy(src, half, send_o.at[0], inner).wait_recv()

    def got_e(k):
        e_copy(k, send_o.at[0], inner).wait_recv()

    def own_p(half, sem, to):
        return p_copy(me, half, sem, to)

    barrier = pltpu.get_barrier_semaphore()
    pl.semaphore_signal(barrier, inc=1, device_id={"ctx": inner}, device_id_type=MESH)

    @pl.when(is_mid)
    def _():
        pl.semaphore_signal(barrier, inc=1, device_id={"ctx": near}, device_id_type=MESH)

    pb[me] = p_ref[...]
    rb[me, 0] = r_ref[:BLK]
    rb[me, 1] = r_ref[BLK:]

    @pl.when(is_mid)
    def _():
        pl.semaphore_wait(barrier, 2)

    @pl.when(is_end)
    def _():
        pl.semaphore_wait(barrier, 1)

    def send_own(half):
        own_p(half, send_o.at[half], inner).start()

        @pl.when(is_mid)
        def _():
            own_p(half, send_e.at[half], near).start()

    send_own(0)

    def needs(target, cand):
        same = resp_ref[target] == resp_ref[cand]
        return jnp.where(same & (pos_ref[cand] < pos_ref[target]), 1, 0)

    def right_aligned(flags, count):
        after = 0
        ranks = []
        for flag in reversed(flags):
            ranks.append(count - 1 - after)
            after = after + flag
        ranks.reverse()
        return [
            [jnp.where(ranks[i] == k, flags[i], 0) for i in range(len(flags))]
            for k in range(count)
        ]

    def choose(pick, blocks):
        out = blocks[0]
        for i in range(1, len(blocks)):
            out = lax.select_n(pick[i] == 1, out, blocks[i])
        return out

    def end_picks(end, first, second, third):
        cands = [2 * first, 2 * first + 1, 2 * second, 2 * second + 1, 2 * third, 2 * third + 1]
        flags = [jnp.maximum(needs(2 * end, c), needs(2 * end + 1, c)) for c in cands]
        return cands, right_aligned(flags, 4)

    def send_entry(k, sem):
        order = (me, other, far)
        _, picks = end_picks(near, *order)
        blocks = [rb[src, half] for src in order for half in range(2)][: k + 3]
        eb[k] = choose(picks[k], blocks)
        e_copy(k, sem, near).start()

    def attend(k, v, base, bias=None, diag=False):
        keys = k.shape[0]
        k2 = jnp.concatenate([k, k], axis=1)
        scores = [
            lax.dot_general(k2, q2[base + u], NT, preferred_element_type=jnp.float32)
            for u in range(QH // KVH)
        ]
        if diag:
            key_at = lax.broadcasted_iota(jnp.int32, (keys, BLK), 0)
            row_at = lax.broadcasted_iota(jnp.int32, (keys, BLK), 1)
            seen = key_at <= row_at
        for u, s in enumerate(scores):
            i = base + u
            if diag:
                s = jnp.where(seen, s, -1e30)
            peak = jnp.max(s, axis=0, keepdims=True)
            if diag:
                expo = jnp.exp2(s - peak)
                l[i, 0:1] = jnp.sum(expo, axis=0, keepdims=True)
                m[i, 0:1] = peak
                acc[i] = lax.dot_general(
                    v, expo.astype(jnp.bfloat16), TN, preferred_element_type=jnp.float32
                )
            else:
                before = m[i, 0:1]
                if bias is not None:
                    peak = peak - bias
                peak = jnp.maximum(before, peak)
                expo = jnp.exp2(s - (peak if bias is None else peak + bias))
                decay = jnp.exp2(before - peak)
                l[i, 0:1] = l[i, 0:1] * decay + jnp.sum(expo, axis=0, keepdims=True)
                m[i, 0:1] = peak
                acc[i] = acc[i] * decay + lax.dot_general(
                    v, expo.astype(jnp.bfloat16), TN, preferred_element_type=jnp.float32
                )

    def columns(head):
        return (
            pl.ds(pl.multiple_of(head * 2 * HD, 2 * HD), HD),
            pl.ds(pl.multiple_of(head * 2 * HD + HD, HD), HD),
        )

    def q_at(i):
        slot, head = i // 16, i % 16
        return (
            pl.ds(pl.multiple_of(slot * BLK, BLK), BLK),
            pl.ds(pl.multiple_of(head * HD, HD), HD),
        )

    @pl.loop(0, 32)
    def _(i):
        rows, cols = q_at(i)
        scaled = q_ref[rows, cols].astype(jnp.float32) * C2
        high = scaled.astype(jnp.bfloat16)
        rest = (scaled - high.astype(jnp.float32)).astype(jnp.bfloat16)
        q2[i] = jnp.concatenate([high, rest], axis=1)

    send_own(1)

    def own_r(half):
        own_p(half, send_o.at[half], inner).wait_send()
        r_copy(me, half, send_o.at[2 + half], inner).start()

    def event_early(half):
        own_r(half)

        @pl.when(is_mid)
        def _():
            got_p(other, half)
            p_copy(other, half, send_e.at[2 + half], near).start()

    def event_entry(half):
        r_copy(me, half, send_o.at[2 + half], inner).wait_send()
        got_p(near, half)
        p_copy(near, half, send_o.at[4 + half], other).start()
        got_r(other, half)
        send_entry(half, send_e.at[4 + half])

    def event_far_p(half):
        p_copy(near, half, send_o.at[4 + half], other).wait_send()
        got_r(near, half)
        r_copy(near, half, send_o.at[6 + half], other).start()
        got_p(far, half)
        p_copy(far, half, send_e.at[6 + half], near).start()

    def event_far_r(half):
        got_r(far, half)
        send_entry(2 + half, send_e.at[8 + half])

    @pl.loop(0, 4)
    def _(it):
        pl.when(it == 2)(lambda: event_early(0))
        slot, head = it // 2, it % 2
        kc, vc = columns(head)
        rows = pl.ds(pl.multiple_of(slot * BLK, BLK), BLK)
        attend(r_ref[rows, kc], r_ref[rows, vc], slot * 16 + head * 8, diag=True)

    def at(it, tick, role, action):
        pl.when((it == tick) & role)(action)

    def take_p(src):
        def go():
            got_p(src, 0)
            got_p(src, 1)
        return go

    def prompt_step(it):
        step = it // 4
        second = jnp.where(is_end, inner, other)
        third = jnp.where(is_end, jnp.where(low, 2, 1), near)
        fourth = jnp.where(low, 3, 0)
        src = jnp.where(
            step == 0, me, jnp.where(step == 1, second, jnp.where(step == 2, third, fourth))
        )
        pl.when(it == 1)(lambda: event_early(1))
        at(it, 3, is_mid, lambda: event_entry(0))
        at(it, 6, is_mid, lambda: event_entry(1))
        at(it, 9, is_mid, lambda: event_far_p(0))
        at(it, 13, is_mid, lambda: event_far_r(0))
        at(it, 15, is_mid, lambda: event_far_r(1))
        at(it, 4, is_end, take_p(second))
        at(it, 8, is_end, take_p(third))
        at(it, 12, is_end, take_p(fourth))
        slot, head = (it % 4) // 2, it % 2
        kc, vc = columns(head)
        attend(pb[src, :, kc], pb[src, :, vc], slot * 16 + head * 8)

    def fill(k):
        used = []
        for slot in range(2):
            mine, sib = 2 * me + slot, 2 * me + 1 - slot

            order = (near, other, far)
            cands = [2 * src + half for src in order for half in range(2)]
            flags = [needs(mine, sib)] + [needs(mine, c) for c in cands]
            mid_pick = right_aligned(flags, 3)[k]

            ends, picks = end_picks(me, inner, jnp.where(low, 2, 1), jnp.where(low, 3, 0))
            flags = [needs(mine, sib)]
            for entry in range(4):
                flag = 0
                for i, c in enumerate(ends):
                    flag = flag + picks[entry][i] * needs(mine, c)
                flags.append(flag)
            end_pick = right_aligned(flags, 3)[k]

            def fill_mid():
                blocks = [rb[me, 1 - slot]]
                blocks += [rb[src, half] for src in order for half in range(2)][: k + 4]
                fb[slot] = choose(mid_pick, blocks)

            def fill_end():
                blocks = [rb[me, 1 - slot]] + [eb[entry] for entry in range(k + 2)]
                fb[slot] = choose(end_pick, blocks)

            pl.when(is_mid)(fill_mid)
            pl.when(is_end)(fill_end)
            used.append(jnp.where(is_mid, sum(mid_pick), sum(end_pick)))
        biases = [jnp.where(u == 1, 0.0, 1e30).astype(jnp.float32) for u in used]

        @pl.loop(0, 4)
        def _(it):
            slot, head = it // 2, it % 2
            kc, vc = columns(head)
            bias = jnp.where(slot == 0, biases[0], biases[1])
            attend(fb[slot, :, kc], fb[slot, :, vc], slot * 16 + head * 8, bias=bias)

    pl.loop(0, 12)(prompt_step)

    @pl.when(is_end)
    def _():
        got_e(0)
        got_e(1)

    pl.when(is_mid)(lambda: event_far_p(1))
    fill(0)
    pl.loop(12, 16)(prompt_step)
    pl.when(is_end)(lambda: got_e(2))
    fill(1)
    pl.when(is_end)(lambda: got_e(3))
    fill(2)

    @pl.loop(0, 32)
    def _(i):
        o_ref[i] = (acc[i] / l[i, 0:1]).astype(o_ref.dtype)

    @pl.when(is_end)
    def _():
        for half in range(2):
            r_copy(me, half, send_o.at[2 + half], inner).wait_send()

    @pl.when(is_mid)
    def _():
        for half in range(2):
            own_p(half, send_e.at[half], near).wait_send()
            p_copy(other, half, send_e.at[2 + half], near).wait_send()
            e_copy(half, send_e.at[4 + half], near).wait_send()
            p_copy(far, half, send_e.at[6 + half], near).wait_send()
            e_copy(2 + half, send_e.at[8 + half], near).wait_send()
            r_copy(near, half, send_o.at[6 + half], other).wait_send()


def turn(x_ref, o_ref):
    for u in range(x_ref.shape[0]):
        o_ref[:, u * HD : (u + 1) * HD] = x_ref[u].T


def line_of_four(queries, prompt_kv, resp_kv, block_resp, block_pos):
    rows, cols = queries.shape
    width = prompt_kv.shape[1]
    vmem = pl.BlockSpec(memory_space=pltpu.VMEM)
    smem = pl.BlockSpec(memory_space=pltpu.SMEM)
    heads = cols // HD
    tiles = rows // BLK * heads
    turned = pl.pallas_call(
        kernel,
        out_shape=jax.ShapeDtypeStruct((tiles, HD, BLK), jnp.bfloat16),
        in_specs=[vmem, vmem, vmem, smem, smem],
        out_specs=vmem,
        scratch_shapes=[
            pltpu.VMEM((4, 2 * BLK, width), jnp.bfloat16),
            pltpu.VMEM((4, 2, BLK, width), jnp.bfloat16),
            pltpu.VMEM((4, BLK, width), jnp.bfloat16),
            pltpu.VMEM((2, BLK, width), jnp.bfloat16),
            pltpu.VMEM((tiles, BLK, 2 * HD), jnp.bfloat16),
            pltpu.VMEM((tiles, HD, BLK), jnp.float32),
            pltpu.VMEM((tiles, 8, BLK), jnp.float32),
            pltpu.VMEM((tiles, 8, BLK), jnp.float32),
            pltpu.SemaphoreType.DMA((4, 2)),
            pltpu.SemaphoreType.DMA((4, 2)),
            pltpu.SemaphoreType.DMA((4,)),
            pltpu.SemaphoreType.DMA((10,)),
            pltpu.SemaphoreType.DMA((8,)),
        ],
        compiler_params=pltpu.CompilerParams(
            collective_id=0, has_side_effects=True, vmem_limit_bytes=56 * 2**20
        ),
        name="line_attention",
    )(queries, prompt_kv, resp_kv, block_resp, block_pos)
    some = heads // 2
    return pl.pallas_call(
        turn,
        grid=(tiles // some,),
        out_shape=jax.ShapeDtypeStruct((rows, cols), jnp.bfloat16),
        in_specs=[pl.BlockSpec((some, HD, BLK), lambda i: (i, 0, 0))],
        out_specs=pl.BlockSpec((BLK, some * HD), lambda i: (i // 2, i % 2)),
        name="turn",
    )(turned)


def shards_of(queries, prompt_kv, resp_kv, block_resp, block_pos):
    ctx = lax.axis_size("ctx")
    fits = (
        ctx == 4
        and queries.shape == (2 * BLK, 2 * (QH // KVH) * HD)
        and prompt_kv.shape == (PLEN // 4, 4 * HD)
        and resp_kv.shape == (2 * BLK, 4 * HD)
    )
    run = line_of_four if fits else shards
    return run(queries, prompt_kv, resp_kv, block_resp, block_pos)


def solution(mesh):
    in_specs = (
        P(("groups", "ctx"), ("tp", "sub")),
        P(("groups", "ctx"), ("tp", "sub")),
        P(("groups", "ctx"), ("tp", "sub")),
        P("groups"),
        P("groups"),
    )
    out_specs = P(("groups", "ctx"), ("tp", "sub"))
    return jax.shard_map(shards_of, mesh=mesh, in_specs=in_specs, out_specs=out_specs, check_vma=False)
```

```python
import math

import jax
import jax.numpy as jnp
from jax import lax
from jax.experimental import pallas as pl
from jax.experimental.pallas import tpu as pltpu
from jax.sharding import PartitionSpec as P

HD = 128
QH = 64
KVH = 8
BLK = 256
PLEN = 2048
GEN = 4
MAXB = 4


def shards(queries, prompt_kv, resp_kv, block_resp, block_pos):
    rows = queries.shape[0]
    nloc = rows // BLK
    width = prompt_kv.shape[1]
    kvloc = width // (2 * HD)
    group = QH // KVH
    qloc = kvloc * group
    nblk = block_resp.shape[0]
    scale = 1.0 / math.sqrt(HD)
    slots_here = lax.axis_index("ctx") * nloc + jnp.arange(nloc, dtype=jnp.int32)
    resp_here = block_resp[slots_here]
    pos_here = block_pos[slots_here]
    qheads = queries.reshape(nloc, BLK, qloc, HD).transpose(2, 0, 1, 3)
    within = jnp.arange(BLK, dtype=jnp.int32)
    all_prompt, all_answer = (
        lax.all_gather(prompt_kv, "ctx", axis=0, tiled=True),
        lax.all_gather(resp_kv, "ctx", axis=0, tiled=True),
    )
    answer_blocks = all_answer.reshape(nblk, BLK, width)
    positions = jnp.arange(MAXB, dtype=jnp.int32)
    hit = (block_resp[None, None, :] == resp_here[:, None, None]) & (
        block_pos[None, None, :] == positions[None, :, None]
    )
    table = jnp.sum(jnp.where(hit, jnp.arange(nblk, dtype=jnp.int32)[None, None, :], 0), axis=-1)
    prompt_rows = jnp.stack(
        [
            lax.dynamic_slice_in_dim(all_prompt, resp_here[slot] // GEN * PLEN, PLEN, 0)
            for slot in range(nloc)
        ]
    )
    answer_rows = answer_blocks[table].reshape(nloc, MAXB * BLK, width)
    keyvals = jnp.concatenate([prompt_rows, answer_rows], axis=1).reshape(
        nloc, PLEN + MAXB * BLK, kvloc, 2, HD
    )
    keys = keyvals[:, :, :, 0].transpose(2, 0, 1, 3)
    values = keyvals[:, :, :, 1].transpose(2, 0, 1, 3)
    which = jnp.repeat(positions, BLK)
    inner = jnp.tile(within, MAXB)
    answer_mask = (which[None, None, :] < pos_here[:, None, None]) | (
        which[None, None, :] == pos_here[:, None, None]
    ) & (inner[None, None, :] <= within[None, :, None])
    mask = jnp.concatenate([jnp.ones((nloc, BLK, PLEN), dtype=bool), answer_mask], axis=2)

    def one_head(index):
        owner = index // group
        scores = (
            jnp.einsum(
                "btd,bld->btl", qheads[index], keys[owner], preferred_element_type=jnp.float32
            )
            * scale
        )
        scores = jnp.where(mask, scores, -1e30)
        peak = jnp.max(scores, axis=-1, keepdims=True)
        expo = jnp.exp(scores - peak)
        total = jnp.sum(expo, axis=-1, keepdims=True)
        probs = expo.astype(jnp.bfloat16)
        mixed = (
            jnp.einsum("btl,bld->btd", probs, values[owner], preferred_element_type=jnp.float32)
            / total
        )
        return mixed.astype(jnp.bfloat16)

    outputs = lax.map(one_head, jnp.arange(qloc, dtype=jnp.int32))
    return outputs.transpose(1, 2, 0, 3).reshape(rows, qloc * HD)


NT = (((1,), (1,)), ((), ()))
TN = (((0,), (0,)), ((), ()))
C2 = math.log2(math.e) / math.sqrt(HD)
MESH = pl.DeviceIdType.MESH


def kernel(
    q_ref, p_ref, r_ref, resp_ref, pos_ref, o_ref,
    pb, rb, eb, fb, q2, acc, m, l,
    recv_p, recv_r, recv_e, send_e, send_o,
):
    me = lax.axis_index("ctx")
    is_end = (me == 0) | (me == 3)
    is_mid = (me == 1) | (me == 2)
    low = me < 2
    near = jnp.where(low, 0, 3)
    other = jnp.where(low, 2, 1)
    far = 3 - near
    inner = jnp.where(me == 0, 1, jnp.where(me == 3, 2, other))

    def p_at(src, half):
        return pb.at[src, pl.ds(half * BLK, BLK)]

    def p_copy(src, half, sem, to):
        return pltpu.make_async_remote_copy(
            src_ref=p_at(src, half), dst_ref=p_at(src, half), send_sem=sem,
            recv_sem=recv_p.at[src, half], device_id={"ctx": to}, device_id_type=MESH,
        )

    def r_copy(src, half, sem, to):
        return pltpu.make_async_remote_copy(
            src_ref=rb.at[src, half], dst_ref=rb.at[src, half], send_sem=sem,
            recv_sem=recv_r.at[src, half], device_id={"ctx": to}, device_id_type=MESH,
        )

    def e_copy(k, sem, to):
        return pltpu.make_async_remote_copy(
            src_ref=eb.at[k], dst_ref=eb.at[k], send_sem=sem,
            recv_sem=recv_e.at[k], device_id={"ctx": to}, device_id_type=MESH,
        )

    def got_p(src, half):
        p_copy(src, half, send_o.at[0], inner).wait_recv()

    def got_r(src, half):
        r_copy(src, half, send_o.at[0], inner).wait_recv()

    def got_e(k):
        e_copy(k, send_o.at[0], inner).wait_recv()

    def own_p(half, sem, to):
        return p_copy(me, half, sem, to)

    barrier = pltpu.get_barrier_semaphore()
    pl.semaphore_signal(barrier, inc=1, device_id={"ctx": inner}, device_id_type=MESH)

    @pl.when(is_mid)
    def _():
        pl.semaphore_signal(barrier, inc=1, device_id={"ctx": near}, device_id_type=MESH)

    pb[me] = p_ref[...]
    rb[me, 0] = r_ref[:BLK]
    rb[me, 1] = r_ref[BLK:]

    @pl.when(is_mid)
    def _():
        pl.semaphore_wait(barrier, 2)

    @pl.when(is_end)
    def _():
        pl.semaphore_wait(barrier, 1)

    def send_own(half):
        own_p(half, send_o.at[half], inner).start()

        @pl.when(is_mid)
        def _():
            own_p(half, send_e.at[half], near).start()

    send_own(0)

    def needs(target, cand):
        same = resp_ref[target] == resp_ref[cand]
        return jnp.where(same & (pos_ref[cand] < pos_ref[target]), 1, 0)

    def right_aligned(flags, count):
        after = 0
        ranks = []
        for flag in reversed(flags):
            ranks.append(count - 1 - after)
            after = after + flag
        ranks.reverse()
        return [
            [jnp.where(ranks[i] == k, flags[i], 0) for i in range(len(flags))]
            for k in range(count)
        ]

    def choose(pick, blocks):
        out = blocks[0]
        for i in range(1, len(blocks)):
            out = lax.select_n(pick[i] == 1, out, blocks[i])
        return out

    def end_picks(end, first, second, third):
        cands = [2 * first, 2 * first + 1, 2 * second, 2 * second + 1, 2 * third, 2 * third + 1]
        flags = [jnp.maximum(needs(2 * end, c), needs(2 * end + 1, c)) for c in cands]
        return cands, right_aligned(flags, 4)

    def send_entry(k, sem):
        order = (me, other, far)
        _, picks = end_picks(near, *order)
        blocks = [rb[src, half] for src in order for half in range(2)][: k + 3]
        eb[k] = choose(picks[k], blocks)
        e_copy(k, sem, near).start()

    def attend(k, v, base, bias=None, diag=False):
        keys = k.shape[0]
        k2 = jnp.concatenate([k, k], axis=1)
        scores = [
            lax.dot_general(k2, q2[base + u], NT, preferred_element_type=jnp.float32)
            for u in range(QH // KVH)
        ]
        if diag:
            key_at = lax.broadcasted_iota(jnp.int32, (keys, BLK), 0)
            row_at = lax.broadcasted_iota(jnp.int32, (keys, BLK), 1)
            seen = key_at <= row_at
        for u, s in enumerate(scores):
            i = base + u
            if diag:
                s = jnp.where(seen, s, -1e30)
            peak = jnp.max(s, axis=0, keepdims=True)
            if diag:
                expo = jnp.exp2(s - peak)
                l[i, 0:1] = jnp.sum(expo, axis=0, keepdims=True)
                m[i, 0:1] = peak
                acc[i] = lax.dot_general(
                    v, expo.astype(jnp.bfloat16), TN, preferred_element_type=jnp.float32
                )
            else:
                before = m[i, 0:1]
                if bias is not None:
                    peak = peak - bias
                peak = jnp.maximum(before, peak)
                expo = jnp.exp2(s - (peak if bias is None else peak + bias))
                decay = jnp.exp2(before - peak)
                l[i, 0:1] = l[i, 0:1] * decay + jnp.sum(expo, axis=0, keepdims=True)
                m[i, 0:1] = peak
                acc[i] = acc[i] * decay + lax.dot_general(
                    v, expo.astype(jnp.bfloat16), TN, preferred_element_type=jnp.float32
                )

    def columns(head):
        return (
            pl.ds(pl.multiple_of(head * 2 * HD, 2 * HD), HD),
            pl.ds(pl.multiple_of(head * 2 * HD + HD, HD), HD),
        )

    def q_at(i):
        slot, head = i // 16, i % 16
        return (
            pl.ds(pl.multiple_of(slot * BLK, BLK), BLK),
            pl.ds(pl.multiple_of(head * HD, HD), HD),
        )

    @pl.loop(0, 32)
    def _(i):
        rows, cols = q_at(i)
        scaled = q_ref[rows, cols].astype(jnp.float32) * C2
        high = scaled.astype(jnp.bfloat16)
        rest = (scaled - high.astype(jnp.float32)).astype(jnp.bfloat16)
        q2[i] = jnp.concatenate([high, rest], axis=1)

    send_own(1)

    def own_r(half):
        own_p(half, send_o.at[half], inner).wait_send()
        r_copy(me, half, send_o.at[2 + half], inner).start()

    def event_early(half):
        own_r(half)

        @pl.when(is_mid)
        def _():
            got_p(other, half)
            p_copy(other, half, send_e.at[2 + half], near).start()

    def event_entry(half):
        r_copy(me, half, send_o.at[2 + half], inner).wait_send()
        got_p(near, half)
        p_copy(near, half, send_o.at[4 + half], other).start()
        got_r(other, half)
        send_entry(half, send_e.at[4 + half])

    def event_far_p(half):
        p_copy(near, half, send_o.at[4 + half], other).wait_send()
        got_r(near, half)
        r_copy(near, half, send_o.at[6 + half], other).start()
        got_p(far, half)
        p_copy(far, half, send_e.at[6 + half], near).start()

    def event_far_r(half):
        got_r(far, half)
        send_entry(2 + half, send_e.at[8 + half])

    @pl.loop(0, 4)
    def _(it):
        pl.when(it == 2)(lambda: event_early(0))
        slot, head = it // 2, it % 2
        kc, vc = columns(head)
        rows = pl.ds(pl.multiple_of(slot * BLK, BLK), BLK)
        attend(r_ref[rows, kc], r_ref[rows, vc], slot * 16 + head * 8, diag=True)

    def at(it, tick, role, action):
        pl.when((it == tick) & role)(action)

    def take_p(src):
        def go():
            got_p(src, 0)
            got_p(src, 1)
        return go

    def prompt_step(it):
        step = it // 4
        second = jnp.where(is_end, inner, other)
        third = jnp.where(is_end, jnp.where(low, 2, 1), near)
        src = jnp.where(step == 0, me, jnp.where(step == 1, second, third))
        pl.when(it == 1)(lambda: event_early(1))
        at(it, 3, is_mid, lambda: event_entry(0))
        at(it, 6, is_mid, lambda: event_entry(1))
        at(it, 9, is_mid, lambda: event_far_p(0))
        at(it, 4, is_end, take_p(second))
        at(it, 8, is_end, take_p(third))
        slot, head = (it % 4) // 2, it % 2
        kc, vc = columns(head)
        attend(pb[src, :, kc], pb[src, :, vc], slot * 16 + head * 8)

    def last_step(it):
        half = it // 4
        src = jnp.where(low, 3, 0)
        at(it, 0, is_end, lambda: got_p(src, 0))
        at(it, 4, is_end, lambda: got_p(src, 1))
        at(it, 2, is_mid, lambda: event_far_r(0))
        at(it, 5, is_mid, lambda: event_far_r(1))
        slot, head = (it % 4) // 2, it % 2
        kc, vc = columns(head)
        rows = pl.ds(pl.multiple_of(half * BLK, BLK), BLK)
        attend(pb[src, rows, kc], pb[src, rows, vc], slot * 16 + head * 8)

    def fill(k):
        used = []
        for slot in range(2):
            mine, sib = 2 * me + slot, 2 * me + 1 - slot

            order = (near, other, far)
            cands = [2 * src + half for src in order for half in range(2)]
            flags = [needs(mine, sib)] + [needs(mine, c) for c in cands]
            mid_pick = right_aligned(flags, 3)[k]

            ends, picks = end_picks(me, inner, jnp.where(low, 2, 1), jnp.where(low, 3, 0))
            flags = [needs(mine, sib)]
            for entry in range(4):
                flag = 0
                for i, c in enumerate(ends):
                    flag = flag + picks[entry][i] * needs(mine, c)
                flags.append(flag)
            end_pick = right_aligned(flags, 3)[k]

            def fill_mid():
                blocks = [rb[me, 1 - slot]]
                blocks += [rb[src, half] for src in order for half in range(2)][: k + 4]
                fb[slot] = choose(mid_pick, blocks)

            def fill_end():
                blocks = [rb[me, 1 - slot]] + [eb[entry] for entry in range(k + 2)]
                fb[slot] = choose(end_pick, blocks)

            pl.when(is_mid)(fill_mid)
            pl.when(is_end)(fill_end)
            used.append(jnp.where(is_mid, sum(mid_pick), sum(end_pick)))
        biases = [jnp.where(u == 1, 0.0, 1e30).astype(jnp.float32) for u in used]

        @pl.loop(0, 4)
        def _(it):
            slot, head = it // 2, it % 2
            kc, vc = columns(head)
            bias = jnp.where(slot == 0, biases[0], biases[1])
            attend(fb[slot, :, kc], fb[slot, :, vc], slot * 16 + head * 8, bias=bias)

    pl.loop(0, 12)(prompt_step)

    @pl.when(is_end)
    def _():
        got_e(0)
        got_e(1)

    pl.when(is_mid)(lambda: event_far_p(1))
    fill(0)
    pl.loop(0, 8)(last_step)
    pl.when(is_end)(lambda: got_e(2))
    fill(1)
    pl.when(is_end)(lambda: got_e(3))
    fill(2)

    @pl.loop(0, 32)
    def _(i):
        o_ref[i] = (acc[i] / l[i, 0:1]).astype(o_ref.dtype)

    @pl.when(is_end)
    def _():
        for half in range(2):
            r_copy(me, half, send_o.at[2 + half], inner).wait_send()

    @pl.when(is_mid)
    def _():
        for half in range(2):
            own_p(half, send_e.at[half], near).wait_send()
            p_copy(other, half, send_e.at[2 + half], near).wait_send()
            e_copy(half, send_e.at[4 + half], near).wait_send()
            p_copy(far, half, send_e.at[6 + half], near).wait_send()
            e_copy(2 + half, send_e.at[8 + half], near).wait_send()
            r_copy(near, half, send_o.at[6 + half], other).wait_send()


def turn(x_ref, o_ref):
    for u in range(x_ref.shape[0]):
        o_ref[:, u * HD : (u + 1) * HD] = x_ref[u].T


def line_of_four(queries, prompt_kv, resp_kv, block_resp, block_pos):
    rows, cols = queries.shape
    width = prompt_kv.shape[1]
    vmem = pl.BlockSpec(memory_space=pltpu.VMEM)
    smem = pl.BlockSpec(memory_space=pltpu.SMEM)
    heads = cols // HD
    tiles = rows // BLK * heads
    turned = pl.pallas_call(
        kernel,
        out_shape=jax.ShapeDtypeStruct((tiles, HD, BLK), jnp.bfloat16),
        in_specs=[vmem, vmem, vmem, smem, smem],
        out_specs=vmem,
        scratch_shapes=[
            pltpu.VMEM((4, 2 * BLK, width), jnp.bfloat16),
            pltpu.VMEM((4, 2, BLK, width), jnp.bfloat16),
            pltpu.VMEM((4, BLK, width), jnp.bfloat16),
            pltpu.VMEM((2, BLK, width), jnp.bfloat16),
            pltpu.VMEM((tiles, BLK, 2 * HD), jnp.bfloat16),
            pltpu.VMEM((tiles, HD, BLK), jnp.float32),
            pltpu.VMEM((tiles, 8, BLK), jnp.float32),
            pltpu.VMEM((tiles, 8, BLK), jnp.float32),
            pltpu.SemaphoreType.DMA((4, 2)),
            pltpu.SemaphoreType.DMA((4, 2)),
            pltpu.SemaphoreType.DMA((4,)),
            pltpu.SemaphoreType.DMA((10,)),
            pltpu.SemaphoreType.DMA((8,)),
        ],
        compiler_params=pltpu.CompilerParams(
            collective_id=0, has_side_effects=True, vmem_limit_bytes=56 * 2**20
        ),
        name="line_attention",
    )(queries, prompt_kv, resp_kv, block_resp, block_pos)
    some = heads // 2
    return pl.pallas_call(
        turn,
        grid=(tiles // some,),
        out_shape=jax.ShapeDtypeStruct((rows, cols), jnp.bfloat16),
        in_specs=[pl.BlockSpec((some, HD, BLK), lambda i: (i, 0, 0))],
        out_specs=pl.BlockSpec((BLK, some * HD), lambda i: (i // 2, i % 2)),
        name="turn",
    )(turned)


def shards_of(queries, prompt_kv, resp_kv, block_resp, block_pos):
    ctx = lax.axis_size("ctx")
    fits = (
        ctx == 4
        and queries.shape == (2 * BLK, 2 * (QH // KVH) * HD)
        and prompt_kv.shape == (PLEN // 4, 4 * HD)
        and resp_kv.shape == (2 * BLK, 4 * HD)
    )
    run = line_of_four if fits else shards
    return run(queries, prompt_kv, resp_kv, block_resp, block_pos)


def solution(mesh):
    in_specs = (
        P(("groups", "ctx"), ("tp", "sub")),
        P(("groups", "ctx"), ("tp", "sub")),
        P(("groups", "ctx"), ("tp", "sub")),
        P("groups"),
        P("groups"),
    )
    out_specs = P(("groups", "ctx"), ("tp", "sub"))
    return jax.shard_map(shards_of, mesh=mesh, in_specs=in_specs, out_specs=out_specs, check_vma=False)
```
